32 devices in a mesh: ctx: 8 (over z, core), head: 4 (over y, x).
Axes of the slice: x: 2, y: 2, z: 4, core: 2. Of those that a mesh axis runs over, the one named last changes fastest.
Arguments:
- queries: bfloat16 [2048, 2048], P('ctx', 'head'), may hold values from -1.1953125 to 1.1953125
- keys: bfloat16 [2048, 2048], P('ctx', 'head'), may hold values from -1.1953125 to 1.1953125
- values: bfloat16 [2048, 2048], P('ctx', 'head'), may hold values from -6 to 6
- log_decay: float32 [2048, 16], P('ctx', 'head'), may hold values from -3 to 0, as said below
- gain: float32 [2048], P('head'), may hold values from 0.1 to 1.9
- grad_normed: bfloat16 [2048, 2048], P('ctx', 'head'), may hold values from -6 to 6
Outputs:
- grad_query: bfloat16 [2048, 2048], P('ctx', 'head')
- grad_key: bfloat16 [2048, 2048], P('ctx', 'head')
- grad_value: bfloat16 [2048, 2048], P('ctx', 'head')
The draws below stay inside these ranges and needn't reach their ends.
Inputs may be any that keep to these rules, and one draw needn't show every extreme that they name: `log_decay`: negative everywhere.
All inputs are finite; a program needn't handle non-finite values.
Results may differ from the reference program's by a relative error of at most 0.0051.
Values sent between devices are 32-bit elements; how exact they have to be, the bound alone decides.
A program may use at most 64 MiB of HBM per device.

```python
import jax
import jax.numpy as jnp
from jax import lax

HD = 128
TOK_DEV = 256
HEADS = 16
FEATS = 2048
TOKENS = 2048


def draw_log_decay(key, part):
    parts = jax.random.split(jax.random.fold_in(key, 17), 6)
    slow_share = 0.5
    slow_pick = jax.random.uniform(parts[0], (HEADS,), jnp.float32) < slow_share
    fast_rate = jax.random.uniform(parts[1], (HEADS,), jnp.float32, 10.0 / TOK_DEV, 16.0 / TOK_DEV)
    slow_rate = jax.random.uniform(parts[2], (HEADS,), jnp.float32, 0.1 / TOKENS, 0.5 / TOKENS)
    rate = jnp.where(slow_pick, slow_rate, fast_rate)
    rough = jax.random.uniform(parts[3], (TOKENS, HEADS), jnp.float32, 0.5, 1.5)
    base = -rate[None, :] * rough
    places = jax.random.randint(parts[4], (3,), 0, TOKENS)
    drops = jax.random.uniform(parts[5], (3, HEADS), jnp.float32, jnp.log(0.55), jnp.log(0.8))
    where_pos = jnp.arange(TOKENS)[:, None] == places[None, :]
    bumps = jnp.sum(jnp.where(where_pos[:, :, None], drops[None, :, :], 0.0), axis=1)
    return (base + bumps).astype(jnp.float32)


def level_of(own_key, extent, shards, least, top_value):
    def one(axis_at, blocks):
        draws = jax.random.uniform(jax.random.fold_in(jax.random.fold_in(own_key, 6), axis_at), (blocks,), jnp.float32, least / len(shards), top_value / len(shards))
        return jnp.repeat(jnp.exp(draws), extent[axis_at] // blocks).reshape((-1,) + (1,) * (len(extent) - axis_at - 1))

    level = one(*shards[0])
    for cut in shards[1:]:
        level = level * one(*cut)
    return level


def normal_values(rng, dims, scale, most, cuts=(), dtype=jnp.bfloat16):
    drawn = jax.random.normal(rng, dims, jnp.float32) * scale
    if len(cuts) > 0:
        drawn = level_of(rng, dims, cuts, -0.22, 0.18) * drawn
    return jnp.clip(drawn, min=-most, max=most).astype(dtype)


def setup_inputs(seed: int = 0) -> dict:
    splits = jax.random.split(jax.random.key(seed), 7)
    return {
        "queries": normal_values(splits[0], (TOKENS, FEATS), 0.2, 1.1953125, ((0, 8), (1, 4))),
        "keys": normal_values(splits[1], (TOKENS, FEATS), 0.2, 1.1953125, ((0, 8), (1, 4))),
        "values": normal_values(splits[2], (TOKENS, FEATS), 1.0, 6.0, ((0, 8), (1, 4))),
        "log_decay": draw_log_decay(jax.random.fold_in(splits[6], 71), 0),
        "gain": jnp.clip(1.0 + 0.18 * jax.random.normal(splits[4], (FEATS,), jnp.float32), 0.1, 1.9),
        "grad_normed": normal_values(splits[5], (TOKENS, FEATS), 1.0, 6.0, ((0, 8), (1, 4))),
    }


def block_decay(logd):
    cum = jnp.cumsum(logd, axis=0)
    last = cum[-1]
    trans = cum.T
    diff = trans[:, :, None] - trans[:, None, :]
    count = logd.shape[0]
    lower = jnp.arange(count)[:, None] >= jnp.arange(count)[None, :]
    decay = jnp.where(lower[None], jnp.exp(jnp.minimum(diff, 0.0)), 0.0)
    return (cum, last, decay)

def reference(queries, keys, values, log_decay, gain, grad_normed):
    blocks = TOKENS // TOK_DEV
    shape4 = (blocks, TOK_DEV, HEADS, HD)
    q_blocks = queries.reshape(shape4)
    k_blocks = keys.reshape(shape4)
    v_blocks = values.reshape(shape4)
    dy_blocks = grad_normed.reshape(shape4)
    l_blocks = log_decay.reshape(blocks, TOK_DEV, HEADS)
    gain3 = gain.reshape(HEADS, HD)
    highest = lax.Precision.HIGHEST

    def states_of(item):
        k_in, v_in, logd = item
        cum = jnp.cumsum(logd, axis=0)
        last = cum[-1]
        weighted = k_in.astype(jnp.float32) * jnp.exp(last[None, :] - cum)[:, :, None]
        state = jnp.einsum('thi,thj->hij', weighted, v_in.astype(jnp.float32), precision=highest)
        return (last, state)
    lasts, bstates = lax.map(states_of, (k_blocks, v_blocks, l_blocks))

    def fwd_step(carry, item):
        last, state = item
        return (jnp.exp(last)[:, None, None] * carry + state, carry)
    zero_state = jnp.zeros((HEADS, HD, HD), jnp.float32)
    _, state_in = lax.scan(fwd_step, zero_state, (lasts, bstates))

    def middle(item):
        q_in, k_in, v_in, logd, dy_in, s_in = item
        cum, last, decay = block_decay(logd)
        q32 = q_in.astype(jnp.float32)
        scores = jnp.einsum('thd,shd->hts', q32, k_in.astype(jnp.float32))
        fwd_w = (scores * decay).astype(jnp.bfloat16)
        attn = jnp.einsum('hts,shd->thd', fwd_w.astype(jnp.float32), v_in.astype(jnp.float32))
        attn = attn + jnp.exp(cum)[:, :, None] * jnp.einsum('thi,hij->thj', q32, s_in, precision=highest)
        dy32 = dy_in.astype(jnp.float32)
        sumsq = lax.optimization_barrier(jnp.sum(attn * attn, axis=(1, 2)))
        cross = lax.optimization_barrier(jnp.sum(gain3[None] * dy32 * attn, axis=(1, 2)))
        rinv = 1.0 / jnp.sqrt(sumsq / FEATS + 1e-06)
        grad_out = gain3[None] * dy32 * rinv[:, None, None] - attn * (cross * rinv ** 3 / FEATS)[:, None, None]
        grad_out = grad_out.astype(jnp.bfloat16)
        qw = q32 * jnp.exp(cum)[:, :, None]
        xgrad = jnp.einsum('thi,thj->hij', qw, grad_out.astype(jnp.float32), precision=highest)
        return (grad_out, xgrad)
    grad_out, xgrads = lax.map(middle, (q_blocks, k_blocks, v_blocks, l_blocks, dy_blocks, state_in))

    def bwd_step(carry, item):
        last, xgrad = item
        return (xgrad + jnp.exp(last)[:, None, None] * carry, carry)
    _, state_grad = lax.scan(bwd_step, zero_state, (lasts, xgrads), reverse=True)

    def final(item):
        q_in, k_in, v_in, logd, go_in, s_in, g_in = item
        cum, last, decay = block_decay(logd)
        q32 = q_in.astype(jnp.float32)
        k32 = k_in.astype(jnp.float32)
        v32 = v_in.astype(jnp.float32)
        go32 = go_in.astype(jnp.float32)
        scores = jnp.einsum('thd,shd->hts', q32, k32)
        fwd_w = (scores * decay).astype(jnp.bfloat16).astype(jnp.float32)
        bwd_w = (jnp.einsum('thd,shd->hts', go32, v32) * decay).astype(jnp.bfloat16).astype(jnp.float32)
        tail = jnp.exp(last[None, :] - cum)[:, :, None]
        grad_q = jnp.einsum('hts,shd->thd', bwd_w, k32)
        grad_q = grad_q + jnp.exp(cum)[:, :, None] * jnp.einsum('thj,hij->thi', go32, s_in, precision=highest)
        grad_k = jnp.einsum('hts,thd->shd', bwd_w, q32)
        grad_k = grad_k + tail * jnp.einsum('thj,hij->thi', v32, g_in, precision=highest)
        grad_v = jnp.einsum('hts,thd->shd', fwd_w, go32)
        grad_v = grad_v + tail * jnp.einsum('thi,hij->thj', k32, g_in, precision=highest)
        return (grad_q.astype(jnp.bfloat16), grad_k.astype(jnp.bfloat16), grad_v.astype(jnp.bfloat16))
    grad_q, grad_k, grad_v = lax.map(final, (q_blocks, k_blocks, v_blocks, l_blocks, grad_out, state_in, state_grad))
    return (grad_q.reshape(TOKENS, FEATS), grad_k.reshape(TOKENS, FEATS), grad_v.reshape(TOKENS, FEATS))
```

```python
import functools

import jax
import jax.numpy as jnp
from jax import lax
from jax.experimental import pallas as pl
from jax.experimental.pallas import tpu as pltpu
from jax.sharding import PartitionSpec as P

F32 = jnp.float32
BF16 = jnp.bfloat16
MESH = pl.DeviceIdType.MESH


def mm(a, b, ca=1, cb=0):
    return lax.dot_general(a, b, (((ca,), (cb,)), ((), ())), preferred_element_type=F32)


def kernel(
    nz, nh, feats_all,
    q, k, v, ld, gain, dy,
    gq, gk, gv,
    own_s, sib_s, state, pass_s, own_x, sib_x, sgrad, pass_x, red_tx, red_rx,
    attn, go, fwd_w, decay, part_k, part_v,
    s_tx, s_rx, e_tx, e_rx, c_tx, c_rx, r_tx, r_rx, x_tx, x_rx, f_tx, f_rx, d_tx, d_rx,
):
    toks = q.shape[0]
    heads = ld.shape[1]
    hd = q.shape[1] // heads
    half = heads // 2
    me = lax.axis_index("ctx")
    grp = lax.axis_index("head")
    z = me // 2
    c = me % 2
    sib = me + 1 - 2 * c
    first = c == 0
    has_prev = z > 0
    has_next = z < nz - 1

    def cols(h):
        return slice(h * hd, (h + 1) * hd)

    def copy(src, dst, tx, rx, where):
        return pltpu.make_async_remote_copy(
            src_ref=src, dst_ref=dst, send_sem=tx, recv_sem=rx,
            device_id=where, device_id_type=MESH,
        )

    barrier = pltpu.get_barrier_semaphore()
    pl.semaphore_signal(barrier, inc=1, device_id={"ctx": sib}, device_id_type=MESH)
    for step in (2, 2 * nz - 2):
        pl.semaphore_signal(
            barrier, inc=1, device_id={"ctx": lax.rem(me + step, 2 * nz)}, device_id_type=MESH
        )
    for d in range(1, nh):
        pl.semaphore_signal(
            barrier, inc=1, device_id={"head": lax.rem(grp + d, nh)}, device_id_type=MESH
        )

    row = lax.broadcasted_iota(jnp.int32, (toks, toks), 0)
    col = lax.broadcasted_iota(jnp.int32, (toks, toks), 1)
    lower = row >= col
    tri = jnp.where(lower, 1.0, 0.0).astype(BF16)
    lane = lax.broadcasted_iota(jnp.int32, (toks, 128), 1)
    logd = jnp.zeros((toks, 128), F32)
    for h in range(heads):
        logd = jnp.where(lane == h, ld[:, h : h + 1], logd)
    high = logd.astype(BF16)
    rest = logd - high.astype(F32)
    mid = rest.astype(BF16)
    low = (rest - mid.astype(F32)).astype(BF16)
    cum = mm(tri, high) + mm(tri, mid) + mm(tri, low)
    last = cum[toks - 1 : toks, :]
    lead_all = jnp.exp(cum)
    tail_all = jnp.exp(last - cum)
    cum_t = cum.T

    for h in range(heads):
        kt = (k[:, cols(h)].astype(F32) * tail_all[:, h : h + 1]).astype(BF16)
        own_s[h, :hd, :] = mm(kt, v[:, cols(h)], 0, 0)
        own_s[h, hd:, :] = jnp.broadcast_to(last[:, h : h + 1], (8, hd))

    pl.semaphore_wait(barrier, 2 + nh)

    def swap(src, dst, tx, rx, h):
        return copy(src.at[h], dst.at[h], tx.at[h], rx.at[h], {"ctx": sib})

    for h in range(heads):
        swap(own_s, sib_s, s_tx, s_rx, h).start()

    @pl.when(jnp.logical_not(has_prev))
    def _():
        state[...] = jnp.zeros_like(state)

    @pl.when(jnp.logical_not(has_next))
    def _():
        sgrad[...] = jnp.zeros_like(sgrad)

    def local(h):
        diff = cum[:, h : h + 1] - cum_t[h : h + 1, :]
        dec = jnp.where(lower, jnp.exp(jnp.minimum(diff, 0.0)), 0.0)
        decay[h] = dec
        w = (mm(q[:, cols(h)], k[:, cols(h)], 1, 1) * dec).astype(BF16)
        fwd_w[h] = w
        attn[:, cols(h)] = mm(w, v[:, cols(h)])

    for h in range(half):
        local(h)
    for h in range(heads):
        swap(own_s, sib_s, s_tx, s_rx, h).wait_recv()

    def pick(own, other, h):
        a = own[h, :hd, :]
        b = other[h, :hd, :]
        return jnp.where(first, a, b), jnp.where(first, b, a)

    def logs(h):
        a = own_s[h, hd : hd + 1, :]
        b = sib_s[h, hd : hd + 1, :]
        return jnp.where(first, a, b), jnp.where(first, b, a)

    def hop(buf, dst, tx, rx, j, step):
        return copy(buf.at[j], dst.at[half * c + j], tx.at[j], rx.at[j], {"ctx": me + step})

    def give(buf, tx, rx, j):
        h = half * c + j
        return copy(buf.at[h], buf.at[h], tx.at[j], rx.at[j], {"ctx": sib})

    def take(buf, tx, rx, j):
        h = half * (1 - c) + j
        return copy(buf.at[h], buf.at[h], tx.at[j], rx.at[j], {"ctx": sib})

    for j in range(half):
        h = half * c + j
        s0, s1 = pick(own_s, sib_s, h)
        l0, l1 = logs(h)
        pass_s[j] = jnp.exp(l1) * s0 + s1

        @pl.when(jnp.logical_not(has_prev) & has_next)
        def _():
            hop(pass_s, state, e_tx, e_rx, j, 2).start()

    for h in range(half, heads):
        local(h)

    @pl.when(has_prev)
    def _():
        for j in range(half):
            h = half * c + j
            hop(pass_s, state, e_tx, e_rx, j, 2).wait_recv()
            give(state, c_tx, c_rx, j).start()

            @pl.when(has_next)
            def _():
                l0, l1 = logs(h)
                pass_s[j] = jnp.exp(l0 + l1) * state[h] + pass_s[j]
                hop(pass_s, state, e_tx, e_rx, j, 2).start()

        for j in range(half):
            take(state, c_tx, c_rx, j).wait_recv()

    sq = jnp.zeros((toks, hd), F32)
    cr = jnp.zeros((toks, hd), F32)
    s_in = []
    for h in range(heads):
        l_sib = sib_s[h, hd : hd + 1, :]
        e = state[h]
        e = jnp.where(first, e, jnp.exp(l_sib) * e + sib_s[h, :hd, :])
        e = e.astype(BF16)
        s_in.append(e)
        a = attn[:, cols(h)] + lead_all[:, h : h + 1] * mm(q[:, cols(h)], e)
        attn[:, cols(h)] = a
        sq = sq + a * a
        cr = cr + gain[:, cols(h)] * dy[:, cols(h)].astype(F32) * a
    sq = jnp.sum(sq, axis=1, keepdims=True)
    cr = jnp.sum(cr, axis=1, keepdims=True)
    both = jnp.where(lane == 0, sq, jnp.where(lane == 1, cr, 0.0)).T
    red_tx[...] = both[:8, :]

    def spread(d):
        return copy(
            red_tx, red_rx.at[d - 1], r_tx.at[d - 1], r_rx.at[d - 1],
            {"head": lax.rem(grp + d, nh)},
        )

    for d in range(1, nh):
        spread(d).start()
    total = red_tx[...]
    for d in range(1, nh):
        spread(d).wait_recv()
        total = total + red_rx[d - 1]
    rinv = 1.0 / jnp.sqrt(total[0:1, :] / feats_all + 1e-06)
    coef = total[1:2, :] * (rinv * rinv * rinv) / feats_all
    sub = lax.broadcasted_iota(jnp.int32, (128, toks), 0)
    scal = jnp.where(sub == 0, rinv, jnp.where(sub == 1, coef, 0.0)).T
    rinv_c = scal[:, 0:1]
    coef_c = scal[:, 1:2]

    for h in range(heads):
        g = gain[:, cols(h)] * dy[:, cols(h)].astype(F32) * rinv_c - attn[:, cols(h)] * coef_c
        g = g.astype(BF16)
        go[:, cols(h)] = g
        ql = (q[:, cols(h)].astype(F32) * lead_all[:, h : h + 1]).astype(BF16)
        own_x[h] = mm(ql, g, 0, 0)
        swap(own_x, sib_x, x_tx, x_rx, h).start()

    def local_back(h):
        g = go[:, cols(h)]
        w = (mm(g, v[:, cols(h)], 1, 1) * decay[h]).astype(BF16)
        out = mm(w, k[:, cols(h)]) + lead_all[:, h : h + 1] * mm(g, s_in[h], 1, 1)
        gq[:, cols(h)] = out.astype(BF16)
        part_k[:, cols(h)] = mm(w, q[:, cols(h)], 0, 0)
        part_v[:, cols(h)] = mm(fwd_w[h], g, 0, 0)

    for h in range(half):
        local_back(h)
    for h in range(heads):
        swap(own_x, sib_x, x_tx, x_rx, h).wait_recv()

    for j in range(half):
        h = half * c + j
        x0, x1 = pick(own_x, sib_x, h)
        l0, l1 = logs(h)
        pass_x[j] = x0 + jnp.exp(l0) * x1

        @pl.when(jnp.logical_not(has_next) & has_prev)
        def _():
            hop(pass_x, sgrad, f_tx, f_rx, j, -2).start()

    for h in range(half, heads):
        local_back(h)

    @pl.when(has_next)
    def _():
        for j in range(half):
            h = half * c + j
            hop(pass_x, sgrad, f_tx, f_rx, j, -2).wait_recv()
            give(sgrad, d_tx, d_rx, j).start()

            @pl.when(has_prev)
            def _():
                l0, l1 = logs(h)
                pass_x[j] = jnp.exp(l0 + l1) * sgrad[h] + pass_x[j]
                hop(pass_x, sgrad, f_tx, f_rx, j, -2).start()

        for j in range(half):
            take(sgrad, d_tx, d_rx, j).wait_recv()

    for h in range(heads):
        l_sib = sib_s[h, hd : hd + 1, :]
        f = sgrad[h]
        f = jnp.where(first, jnp.exp(l_sib) * f + sib_x[h], f).astype(BF16)
        tail = tail_all[:, h : h + 1]
        gk[:, cols(h)] = (part_k[:, cols(h)] + tail * mm(v[:, cols(h)], f, 1, 1)).astype(BF16)
        gv[:, cols(h)] = (part_v[:, cols(h)] + tail * mm(k[:, cols(h)], f)).astype(BF16)

    for h in range(heads):
        swap(own_s, sib_s, s_tx, s_rx, h).wait_send()
        swap(own_x, sib_x, x_tx, x_rx, h).wait_send()
    for d in range(1, nh):
        spread(d).wait_send()

    @pl.when(has_prev)
    def _():
        for j in range(half):
            give(state, c_tx, c_rx, j).wait_send()
            hop(pass_x, sgrad, f_tx, f_rx, j, -2).wait_send()

    @pl.when(has_next)
    def _():
        for j in range(half):
            give(sgrad, d_tx, d_rx, j).wait_send()
            hop(pass_s, state, e_tx, e_rx, j, 2).wait_send()


def on_device(queries, keys, values, log_decay, gain, grad_normed):
    toks, feats = queries.shape
    heads = log_decay.shape[1]
    hd = feats // heads
    half = heads // 2
    nz = lax.axis_size("ctx") // 2
    nh = lax.axis_size("head")
    vm = pl.BlockSpec(memory_space=pltpu.VMEM)
    dma = pltpu.SemaphoreType.DMA
    out = jax.ShapeDtypeStruct((toks, feats), BF16)
    others = max(nh - 1, 1)
    scratch = [
        pltpu.VMEM((heads, hd + 8, hd), F32),
        pltpu.VMEM((heads, hd + 8, hd), F32),
        pltpu.VMEM((heads, hd, hd), F32),
        pltpu.VMEM((half, hd, hd), F32),
        pltpu.VMEM((heads, hd, hd), F32),
        pltpu.VMEM((heads, hd, hd), F32),
        pltpu.VMEM((heads, hd, hd), F32),
        pltpu.VMEM((half, hd, hd), F32),
        pltpu.VMEM((8, toks), F32),
        pltpu.VMEM((others, 8, toks), F32),
        pltpu.VMEM((toks, feats), F32),
        pltpu.VMEM((toks, feats), BF16),
        pltpu.VMEM((heads, toks, toks), BF16),
        pltpu.VMEM((heads, toks, toks), F32),
        pltpu.VMEM((toks, feats), F32),
        pltpu.VMEM((toks, feats), F32),
        dma((heads,)), dma((heads,)),
        dma((half,)), dma((half,)),
        dma((half,)), dma((half,)),
        dma((others,)), dma((others,)),
        dma((heads,)), dma((heads,)),
        dma((half,)), dma((half,)),
        dma((half,)), dma((half,)),
    ]
    return pl.pallas_call(
        functools.partial(kernel, nz, nh, heads * hd * nh),
        out_shape=(out, out, out),
        in_specs=[vm] * 6,
        out_specs=(vm, vm, vm),
        scratch_shapes=scratch,
        compiler_params=pltpu.CompilerParams(
            collective_id=0, has_side_effects=True, vmem_limit_bytes=32 * 1024 * 1024
        ),
    )(queries, keys, values, log_decay, gain.reshape(1, feats), grad_normed)


def solution(mesh):
    in_specs = (
        P("ctx", "head"),
        P("ctx", "head"),
        P("ctx", "head"),
        P("ctx", "head"),
        P("head"),
        P("ctx", "head"),
    )
    out_specs = (P("ctx", "head"), P("ctx", "head"), P("ctx", "head"))
    return jax.shard_map(
        on_device, mesh=mesh, in_specs=in_specs, out_specs=out_specs, check_vma=False
    )
```

```python
import functools

import jax
import jax.numpy as jnp
from jax import lax
from jax.experimental import pallas as pl
from jax.experimental.pallas import tpu as pltpu
from jax.sharding import PartitionSpec as P

F32 = jnp.float32
BF16 = jnp.bfloat16
MESH = pl.DeviceIdType.MESH
CUTS = 2


def mm(a, b, ca=1, cb=0):
    return lax.dot_general(a, b, (((ca,), (cb,)), ((), ())), preferred_element_type=F32)


def kernel(
    nz, nh, feats_all,
    q_h, k_h, v_h, ld_h, gain_h, dy_h,
    gq, gk, gv,
    q, k, v, ld, gain, dy,
    own_s, sib_s, state, pass_s, own_x, sib_x, sgrad, pass_x, red_tx, red_rx,
    attn, go, fwd_w, decay, part_k, part_v, gdy, lead, tail, ql_t, s_in, cum_s,
    in_sem, s_tx, s_rx, e_tx, e_rx, c_tx, c_rx, r_tx, r_rx, x_tx, x_rx, f_tx, f_rx, d_tx, d_rx,
):
    toks = q.shape[0]
    heads = ld.shape[0]
    hd = q.shape[1] // heads
    half = heads // 2
    rows = hd // CUTS
    me = lax.axis_index("ctx")
    grp = lax.axis_index("head")
    z = me // 2
    c = me % 2
    sib = me + 1 - 2 * c
    first = c == 0
    second = c == 1
    has_prev = z > 0
    has_next = z < nz - 1
    from_end = nz - 1 - z

    loads = [
        pltpu.make_async_copy(a, b, in_sem.at[i])
        for i, (a, b) in enumerate(
            ((ld_h, ld), (k_h, k), (v_h, v), (q_h, q), (dy_h, dy), (gain_h, gain))
        )
    ]
    for one in loads:
        one.start()

    def cols(h):
        if isinstance(h, int):
            return slice(h * hd, (h + 1) * hd)
        return pl.ds(pl.multiple_of(h * hd, hd), hd)

    def copy(src, dst, tx, rx, where):
        return pltpu.make_async_remote_copy(
            src_ref=src, dst_ref=dst, send_sem=tx, recv_sem=rx,
            device_id=where, device_id_type=MESH,
        )

    barrier = pltpu.get_barrier_semaphore()
    pl.semaphore_signal(barrier, inc=1, device_id={"ctx": sib}, device_id_type=MESH)
    for step in (2, 2 * nz - 2):
        pl.semaphore_signal(
            barrier, inc=1, device_id={"ctx": lax.rem(me + step, 2 * nz)}, device_id_type=MESH
        )
    for d in range(1, nh):
        pl.semaphore_signal(
            barrier, inc=1, device_id={"head": lax.rem(grp + d, nh)}, device_id_type=MESH
        )

    theirs = [half * (1 - c) + j for j in range(half)]
    mine = [half * c + j for j in range(half)]

    row = lax.broadcasted_iota(jnp.int32, (toks, toks), 0)
    col = lax.broadcasted_iota(jnp.int32, (toks, toks), 1)
    lower = row >= col
    upper = jnp.where(row <= col, 1.0, 0.0).astype(BF16)
    cum_s[...] = jnp.zeros_like(cum_s)
    loads[0].wait()
    logd = ld[...]
    high = logd.astype(BF16)
    rest = logd - high.astype(F32)
    mid = rest.astype(BF16)
    low = (rest - mid.astype(F32)).astype(BF16)
    cum_t = mm(high, upper) + mm(mid, upper) + mm(low, upper)
    cum_s[:heads, :] = cum_t
    cum = cum_s[...].T
    last = cum[toks - 1 : toks, :]
    lead_all = jnp.exp(cum)
    tail_all = jnp.exp(last - cum)
    for h in range(heads):
        tail[h] = jnp.broadcast_to(tail_all[:, h : h + 1], (toks, hd))
        log_h = jnp.broadcast_to(last[:, h : h + 1], (8, hd))
        own_s[h, hd:, :] = log_h
        own_x[h, hd:, :] = log_h
    loads[1].wait()
    loads[2].wait()

    def make_state(h):
        kt = (k[:, cols(h)].astype(F32) * tail[h]).astype(BF16)
        own_s[h, :hd, :] = mm(kt, v[:, cols(h)], 0, 0)

    def swap(src, dst, tx, rx, h, slot):
        return copy(src.at[h], dst.at[h], tx.at[slot], rx.at[slot], {"ctx": sib})

    for j in range(half):
        make_state(theirs[j])
        if j == 0:
            pl.semaphore_wait(barrier, 2 + nh)
        swap(own_s, sib_s, s_tx, s_rx, theirs[j], j).start()
    for j in range(half):
        make_state(mine[j])

        @pl.when(first)
        def _():
            swap(own_s, sib_s, s_tx, s_rx, mine[j], half + j).start()

    @pl.when(jnp.logical_not(has_prev))
    def _():
        state[...] = jnp.zeros_like(state)

    @pl.when(jnp.logical_not(has_next))
    def _():
        sgrad[...] = jnp.zeros_like(sgrad)

    def logs(h):
        a = own_s[h, hd : hd + 1, :]
        b = sib_s[h, hd : hd + 1, :]
        return jnp.where(first, a, b), jnp.where(first, b, a)

    def hop(buf, dst, tx, rx, j, i, step):
        part = pl.ds(i * rows, rows)
        n = j * CUTS + i
        return copy(
            buf.at[j, part], dst.at[mine[j], part], tx.at[n], rx.at[n], {"ctx": me + step}
        )

    def give(buf, tx, rx, j, i):
        part = pl.ds(i * rows, rows)
        n = j * CUTS + i
        return copy(buf.at[mine[j], part], buf.at[mine[j], part], tx.at[n], rx.at[n], {"ctx": sib})

    def take(buf, tx, rx, j, i):
        part = pl.ds(i * rows, rows)
        n = j * CUTS + i
        return copy(
            buf.at[theirs[j], part], buf.at[theirs[j], part], tx.at[n], rx.at[n], {"ctx": sib}
        )

    pieces = [(j, i) for j in range(half) for i in range(CUTS)]

    def chain(buf, dst, tx, rx, g_tx, g_rx, step, onward):
        both = []
        for j in range(half):
            l0, l1 = logs(mine[j])
            both.append(jnp.exp(l0 + l1))
        for j, i in pieces:
            part = pl.ds(i * rows, rows)
            hop(buf, dst, tx, rx, j, i, step).wait_recv()

            @pl.when(onward)
            def _():
                buf[j, part, :] = both[j] * dst[mine[j], part, :] + buf[j, part, :]
                hop(buf, dst, tx, rx, j, i, step).start()

            give(dst, g_tx, g_rx, j, i).start()

    def chain_fwd():
        chain(pass_s, state, e_tx, e_rx, c_tx, c_rx, 2, has_next)

    def chain_back():
        chain(pass_x, sgrad, f_tx, f_rx, d_tx, d_rx, -2, has_prev)

    for j in range(half):
        h = mine[j]
        swap(own_s, sib_s, s_tx, s_rx, h, j).wait_recv()
        l0, l1 = logs(h)
        a = own_s[h, :hd, :]
        b = sib_s[h, :hd, :]
        pass_s[j] = jnp.exp(l1) * jnp.where(first, a, b) + jnp.where(first, b, a)

        @pl.when(jnp.logical_not(has_prev) & has_next)
        def _():
            for i in range(CUTS):
                hop(pass_s, state, e_tx, e_rx, j, i, 2).start()

    @pl.when(z == 1)
    def _():
        chain_fwd()

    for one in loads[3:]:
        one.wait()
    for h in range(heads):
        diff = cum[:, h : h + 1] - cum_t[h : h + 1, :]
        dec = jnp.where(lower, jnp.exp(jnp.minimum(diff, 0.0)), 0.0)
        decay[h] = dec
        w = (mm(q[:, cols(h)], k[:, cols(h)], 1, 1) * dec).astype(BF16)
        fwd_w[h] = w
        attn[:, cols(h)] = mm(w, v[:, cols(h)])
        ahead = jnp.broadcast_to(lead_all[:, h : h + 1], (toks, hd))
        lead[h] = ahead
        ql_t[h] = (q[:, cols(h)].astype(F32) * ahead).astype(BF16).T
        gdy[:, cols(h)] = gain[:, cols(h)] * dy[:, cols(h)].astype(F32)

    @pl.when(z > 1)
    def _():
        chain_fwd()

    @pl.when(second)
    def _():
        for j in range(half):
            swap(own_s, sib_s, s_tx, s_rx, theirs[j], half + j).wait_recv()

    sq = jnp.zeros((toks, hd), F32)
    cr = jnp.zeros((toks, hd), F32)
    for n, h in enumerate(mine + theirs):
        if n >= half:
            @pl.when(has_prev)
            def _():
                for i in range(CUTS):
                    take(state, c_tx, c_rx, n - half, i).wait_recv()

        @pl.when(first)
        def _():
            s_in[h] = state[h].astype(BF16)

        @pl.when(second)
        def _():
            s_in[h] = (
                jnp.exp(sib_s[h, hd : hd + 1, :]) * state[h] + sib_s[h, :hd, :]
            ).astype(BF16)

        a = attn[:, cols(h)] + lead[h] * mm(q[:, cols(h)], s_in[h])
        attn[:, cols(h)] = a
        sq = sq + a * a
        cr = cr + gdy[:, cols(h)] * a
    lane = lax.broadcasted_iota(jnp.int32, (toks, 128), 1)
    sq = jnp.sum(sq, axis=1, keepdims=True)
    cr = jnp.sum(cr, axis=1, keepdims=True)
    both = jnp.where(lane == 0, sq, jnp.where(lane == 1, cr, 0.0)).T
    red_tx[...] = both[:8, :]

    def spread(d):
        return copy(
            red_tx, red_rx.at[d - 1], r_tx.at[d - 1], r_rx.at[d - 1],
            {"head": lax.rem(grp + d, nh)},
        )

    for d in range(1, nh):
        spread(d).start()
    total = red_tx[...]
    for d in range(1, nh):
        spread(d).wait_recv()
        total = total + red_rx[d - 1]
    rinv = 1.0 / jnp.sqrt(total[0:1, :] / feats_all + 1e-06)
    coef = total[1:2, :] * (rinv * rinv * rinv) / feats_all
    sub = lax.broadcasted_iota(jnp.int32, (128, toks), 0)
    scal = jnp.where(sub == 0, rinv, jnp.where(sub == 1, coef, 0.0)).T
    rinv_c = jnp.broadcast_to(scal[:, 0:1], (toks, hd))
    coef_c = jnp.broadcast_to(scal[:, 1:2], (toks, hd))

    def make_grad(h):
        g = (gdy[:, cols(h)] * rinv_c - attn[:, cols(h)] * coef_c).astype(BF16)
        go[:, cols(h)] = g
        own_x[h, :hd, :] = mm(ql_t[h], g)

    for j in range(half):
        make_grad(theirs[j])
        swap(own_x, sib_x, x_tx, x_rx, theirs[j], j).start()
    for j in range(half):
        make_grad(mine[j])

        @pl.when(second)
        def _():
            swap(own_x, sib_x, x_tx, x_rx, mine[j], half + j).start()

    for j in range(half):
        h = mine[j]
        swap(own_x, sib_x, x_tx, x_rx, h, j).wait_recv()
        l0, l1 = logs(h)
        a = own_x[h, :hd, :]
        b = sib_x[h, :hd, :]
        pass_x[j] = jnp.where(first, a, b) + jnp.exp(l0) * jnp.where(first, b, a)

        @pl.when(jnp.logical_not(has_next) & has_prev)
        def _():
            for i in range(CUTS):
                hop(pass_x, sgrad, f_tx, f_rx, j, i, -2).start()

    @pl.when(from_end == 1)
    def _():
        chain_back()

    for h in range(heads):
        g = go[:, cols(h)]
        w = (mm(g, v[:, cols(h)], 1, 1) * decay[h]).astype(BF16)
        out = mm(w, k[:, cols(h)]) + lead[h] * mm(g, s_in[h], 1, 1)
        gq[:, cols(h)] = out.astype(BF16)
        part_k[:, cols(h)] = mm(w, q[:, cols(h)], 0, 0)
        part_v[:, cols(h)] = mm(fwd_w[h], g, 0, 0)

    @pl.when(from_end > 1)
    def _():
        chain_back()

    @pl.when(first)
    def _():
        for j in range(half):
            swap(own_x, sib_x, x_tx, x_rx, theirs[j], half + j).wait_recv()

    for n, h in enumerate(mine + theirs):
        if n >= half:
            @pl.when(has_next)
            def _():
                for i in range(CUTS):
                    take(sgrad, d_tx, d_rx, n - half, i).wait_recv()

        @pl.when(second)
        def _():
            s_in[h] = sgrad[h].astype(BF16)

        @pl.when(first)
        def _():
            s_in[h] = (
                jnp.exp(sib_x[h, hd : hd + 1, :]) * sgrad[h] + sib_x[h, :hd, :]
            ).astype(BF16)

        f = s_in[h]
        gk[:, cols(h)] = (part_k[:, cols(h)] + tail[h] * mm(v[:, cols(h)], f, 1, 1)).astype(BF16)
        gv[:, cols(h)] = (part_v[:, cols(h)] + tail[h] * mm(k[:, cols(h)], f)).astype(BF16)

    for j in range(half):
        swap(own_s, sib_s, s_tx, s_rx, theirs[j], j).wait_send()
        swap(own_x, sib_x, x_tx, x_rx, theirs[j], j).wait_send()

        @pl.when(first)
        def _():
            swap(own_s, sib_s, s_tx, s_rx, mine[j], half + j).wait_send()

        @pl.when(second)
        def _():
            swap(own_x, sib_x, x_tx, x_rx, mine[j], half + j).wait_send()

    for d in range(1, nh):
        spread(d).wait_send()

    @pl.when(has_prev)
    def _():
        for j, i in pieces:
            give(state, c_tx, c_rx, j, i).wait_send()
            hop(pass_x, sgrad, f_tx, f_rx, j, i, -2).wait_send()

    @pl.when(has_next)
    def _():
        for j, i in pieces:
            give(sgrad, d_tx, d_rx, j, i).wait_send()
            hop(pass_s, state, e_tx, e_rx, j, i, 2).wait_send()


def on_device(queries, keys, values, log_decay, gain, grad_normed):
    toks, feats = queries.shape
    heads = log_decay.shape[1]
    hd = feats // heads
    half = heads // 2
    nz = lax.axis_size("ctx") // 2
    nh = lax.axis_size("head")
    vm = pl.BlockSpec(memory_space=pltpu.VMEM)
    hbm = pl.BlockSpec(memory_space=pltpu.HBM)
    dma = pltpu.SemaphoreType.DMA
    out = jax.ShapeDtypeStruct((toks, feats), BF16)
    others = max(nh - 1, 1)
    wide = pltpu.VMEM((toks, feats), BF16)
    wide32 = pltpu.VMEM((toks, feats), F32)
    per_head = pltpu.VMEM((heads, toks, hd), F32)
    tall = pltpu.VMEM((heads, hd + 8, hd), F32)
    full = pltpu.VMEM((heads, hd, hd), F32)
    part = pltpu.VMEM((half, hd, hd), F32)
    links = dma((half * CUTS,))
    scratch = [
        wide, wide, wide, pltpu.VMEM((heads, toks), F32), pltpu.VMEM((1, feats), F32), wide,
        tall, tall, full, part, tall, tall, full, part,
        pltpu.VMEM((8, toks), F32), pltpu.VMEM((others, 8, toks), F32),
        wide32, wide, pltpu.VMEM((heads, toks, toks), BF16),
        pltpu.VMEM((heads, toks, toks), F32), wide32, wide32, wide32,
        per_head, per_head, pltpu.VMEM((heads, hd, toks), BF16),
        pltpu.VMEM((heads, hd, hd), BF16), pltpu.VMEM((128, toks), F32),
        dma((6,)),
        dma((heads,)), dma((heads,)), links, links, links, links,
        dma((others,)), dma((others,)),
        dma((heads,)), dma((heads,)), links, links, links, links,
    ]
    return pl.pallas_call(
        functools.partial(kernel, nz, nh, heads * hd * nh),
        out_shape=(out, out, out),
        in_specs=[hbm] * 6,
        out_specs=(vm, vm, vm),
        scratch_shapes=scratch,
        compiler_params=pltpu.CompilerParams(
            collective_id=0, has_side_effects=True, vmem_limit_bytes=63 * 1024 * 1024
        ),
    )(queries, keys, values, log_decay.T, gain.reshape(1, feats), grad_normed)


def solution(mesh):
    in_specs = (
        P("ctx", "head"),
        P("ctx", "head"),
        P("ctx", "head"),
        P("ctx", "head"),
        P("head"),
        P("ctx", "head"),
    )
    out_specs = (P("ctx", "head"), P("ctx", "head"), P("ctx", "head"))
    return jax.shard_map(
        on_device, mesh=mesh, in_specs=in_specs, out_specs=out_specs, check_vma=False
    )
```

```python
import functools

import jax
import jax.numpy as jnp
from jax import lax
from jax.experimental import pallas as pl
from jax.experimental.pallas import tpu as pltpu
from jax.sharding import PartitionSpec as P

F32 = jnp.float32
BF16 = jnp.bfloat16
MESH = pl.DeviceIdType.MESH
CUTS = 4


def mm(a, b, ca=1, cb=0):
    return lax.dot_general(a, b, (((ca,), (cb,)), ((), ())), preferred_element_type=F32)


def kernel(
    nz, nh, feats_all,
    q_h, k_h, v_h, ld_h, gain_h, dy_h,
    gq, gk, gv,
    q, k, v, ld, gain, dy,
    own_s, sib_s, state, pass_s, own_x, sib_x, sgrad, pass_x, red_tx, red_rx,
    attn, go, fwd_w, decay, part_k, part_v, gdy, lead, tail, ql_t, s_in, cum_s,
    in_sem, s_tx, s_rx, e_tx, e_rx, c_tx, c_rx, r_tx, r_rx, x_tx, x_rx, f_tx, f_rx, d_tx, d_rx,
):
    toks = q.shape[0]
    heads = ld.shape[0]
    hd = q.shape[1] // heads
    half = heads // 2
    rows = hd // CUTS
    me = lax.axis_index("ctx")
    grp = lax.axis_index("head")
    z = me // 2
    c = me % 2
    sib = me + 1 - 2 * c
    first = c == 0
    second = c == 1
    has_prev = z > 0
    has_next = z < nz - 1
    from_end = nz - 1 - z

    loads = [
        pltpu.make_async_copy(a, b, in_sem.at[i])
        for i, (a, b) in enumerate(
            ((ld_h, ld), (k_h, k), (v_h, v), (q_h, q), (dy_h, dy), (gain_h, gain))
        )
    ]
    for one in loads:
        one.start()

    def cols(h):
        if isinstance(h, int):
            return slice(h * hd, (h + 1) * hd)
        return pl.ds(pl.multiple_of(h * hd, hd), hd)

    def copy(src, dst, tx, rx, where):
        return pltpu.make_async_remote_copy(
            src_ref=src, dst_ref=dst, send_sem=tx, recv_sem=rx,
            device_id=where, device_id_type=MESH,
        )

    barrier = pltpu.get_barrier_semaphore()
    pl.semaphore_signal(barrier, inc=1, device_id={"ctx": sib}, device_id_type=MESH)
    for step in (2, 2 * nz - 2):
        pl.semaphore_signal(
            barrier, inc=1, device_id={"ctx": lax.rem(me + step, 2 * nz)}, device_id_type=MESH
        )
    for d in range(1, nh):
        pl.semaphore_signal(
            barrier, inc=1, device_id={"head": lax.rem(grp + d, nh)}, device_id_type=MESH
        )

    theirs = [half * (1 - c) + j for j in range(half)]
    mine = [half * c + j for j in range(half)]

    row = lax.broadcasted_iota(jnp.int32, (toks, toks), 0)
    col = lax.broadcasted_iota(jnp.int32, (toks, toks), 1)
    lower = row >= col
    upper = jnp.where(row <= col, 1.0, 0.0).astype(BF16)
    cum_s[...] = jnp.zeros_like(cum_s)
    loads[0].wait()
    logd = ld[...]
    high = logd.astype(BF16)
    rest = logd - high.astype(F32)
    mid = rest.astype(BF16)
    low = (rest - mid.astype(F32)).astype(BF16)
    cum_t = mm(high, upper) + mm(mid, upper) + mm(low, upper)
    cum_s[:heads, :] = cum_t
    cum = cum_s[...].T
    last = cum[toks - 1 : toks, :]
    lead_all = jnp.exp(cum)
    tail_all = jnp.exp(last - cum)
    for h in range(heads):
        tail[h] = jnp.broadcast_to(tail_all[:, h : h + 1], (toks, hd))
        log_h = jnp.broadcast_to(last[:, h : h + 1], (8, hd))
        own_s[h, hd:, :] = log_h
        own_x[h, hd:, :] = log_h
    loads[1].wait()
    loads[2].wait()

    def make_state(h):
        kt = (k[:, cols(h)].astype(F32) * tail[h]).astype(BF16)
        own_s[h, :hd, :] = mm(kt, v[:, cols(h)], 0, 0)

    def swap(src, dst, tx, rx, h, slot):
        return copy(src.at[h], dst.at[h], tx.at[slot], rx.at[slot], {"ctx": sib})

    for j in range(half):
        make_state(theirs[j])
        if j == 0:
            pl.semaphore_wait(barrier, 2 + nh)
        swap(own_s, sib_s, s_tx, s_rx, theirs[j], j).start()
    for j in range(half):
        make_state(mine[j])

        @pl.when(first)
        def _():
            swap(own_s, sib_s, s_tx, s_rx, mine[j], half + j).start()

    @pl.when(jnp.logical_not(has_prev))
    def _():
        state[...] = jnp.zeros_like(state)

    @pl.when(jnp.logical_not(has_next))
    def _():
        sgrad[...] = jnp.zeros_like(sgrad)

    def logs(h):
        a = own_s[h, hd : hd + 1, :]
        b = sib_s[h, hd : hd + 1, :]
        return jnp.where(first, a, b), jnp.where(first, b, a)

    def hop(buf, dst, tx, rx, j, i, step):
        part = pl.ds(i * rows, rows)
        n = j * CUTS + i
        return copy(
            buf.at[j, part], dst.at[mine[j], part], tx.at[n], rx.at[n], {"ctx": me + step}
        )

    def give(buf, tx, rx, j, i):
        part = pl.ds(i * rows, rows)
        n = j * CUTS + i
        return copy(buf.at[mine[j], part], buf.at[mine[j], part], tx.at[n], rx.at[n], {"ctx": sib})

    def take(buf, tx, rx, j, i):
        part = pl.ds(i * rows, rows)
        n = j * CUTS + i
        return copy(
            buf.at[theirs[j], part], buf.at[theirs[j], part], tx.at[n], rx.at[n], {"ctx": sib}
        )

    pieces = [(j, i) for j in range(half) for i in range(CUTS)]

    def chain(buf, dst, tx, rx, g_tx, g_rx, step, onward):
        both = []
        for j in range(half):
            l0, l1 = logs(mine[j])
            both.append(jnp.exp(l0 + l1))
        for j, i in pieces:
            part = pl.ds(i * rows, rows)
            hop(buf, dst, tx, rx, j, i, step).wait_recv()

            @pl.when(onward)
            def _():
                buf[j, part, :] = both[j] * dst[mine[j], part, :] + buf[j, part, :]
                hop(buf, dst, tx, rx, j, i, step).start()

            give(dst, g_tx, g_rx, j, i).start()

    def chain_fwd():
        chain(pass_s, state, e_tx, e_rx, c_tx, c_rx, 2, has_next)

    def chain_back():
        chain(pass_x, sgrad, f_tx, f_rx, d_tx, d_rx, -2, has_prev)

    for j in range(half):
        h = mine[j]
        swap(own_s, sib_s, s_tx, s_rx, h, j).wait_recv()
        l0, l1 = logs(h)
        a = own_s[h, :hd, :]
        b = sib_s[h, :hd, :]
        pass_s[j] = jnp.exp(l1) * jnp.where(first, a, b) + jnp.where(first, b, a)

        @pl.when(jnp.logical_not(has_prev) & has_next)
        def _():
            for i in range(CUTS):
                hop(pass_s, state, e_tx, e_rx, j, i, 2).start()

    @pl.when(z == 1)
    def _():
        chain_fwd()

    for one in loads[3:]:
        one.wait()
    for h in range(heads):
        diff = cum[:, h : h + 1] - cum_t[h : h + 1, :]
        dec = jnp.where(lower, jnp.exp(jnp.minimum(diff, 0.0)), 0.0)
        decay[h] = dec
        w = (mm(q[:, cols(h)], k[:, cols(h)], 1, 1) * dec).astype(BF16)
        fwd_w[h] = w
        attn[:, cols(h)] = mm(w, v[:, cols(h)])
        ahead = jnp.broadcast_to(lead_all[:, h : h + 1], (toks, hd))
        lead[h] = ahead
        ql_t[h] = (q[:, cols(h)].astype(F32) * ahead).astype(BF16).T
        gdy[:, cols(h)] = gain[:, cols(h)] * dy[:, cols(h)].astype(F32)

    @pl.when(z > 1)
    def _():
        chain_fwd()

    @pl.when(second)
    def _():
        for j in range(half):
            swap(own_s, sib_s, s_tx, s_rx, theirs[j], half + j).wait_recv()

    sq = jnp.zeros((toks, hd), F32)
    cr = jnp.zeros((toks, hd), F32)
    for n, h in enumerate(mine + theirs):
        if n >= half:
            @pl.when(has_prev)
            def _():
                for i in range(CUTS):
                    take(state, c_tx, c_rx, n - half, i).wait_recv()

        @pl.when(first)
        def _():
            s_in[h] = state[h].astype(BF16)

        @pl.when(second)
        def _():
            s_in[h] = (
                jnp.exp(sib_s[h, hd : hd + 1, :]) * state[h] + sib_s[h, :hd, :]
            ).astype(BF16)

        a = attn[:, cols(h)] + lead[h] * mm(q[:, cols(h)], s_in[h])
        attn[:, cols(h)] = a
        sq = sq + a * a
        cr = cr + gdy[:, cols(h)] * a
    lane = lax.broadcasted_iota(jnp.int32, (toks, 128), 1)
    sq = jnp.sum(sq, axis=1, keepdims=True)
    cr = jnp.sum(cr, axis=1, keepdims=True)
    both = jnp.where(lane == 0, sq, jnp.where(lane == 1, cr, 0.0)).T
    red_tx[...] = both[:8, :]

    def spread(d):
        return copy(
            red_tx, red_rx.at[d - 1], r_tx.at[d - 1], r_rx.at[d - 1],
            {"head": lax.rem(grp + d, nh)},
        )

    for d in range(1, nh):
        spread(d).start()
    total = red_tx[...]
    for d in range(1, nh):
        spread(d).wait_recv()
        total = total + red_rx[d - 1]
    rinv = 1.0 / jnp.sqrt(total[0:1, :] / feats_all + 1e-06)
    coef = total[1:2, :] * (rinv * rinv * rinv) / feats_all
    sub = lax.broadcasted_iota(jnp.int32, (128, toks), 0)
    scal = jnp.where(sub == 0, rinv, jnp.where(sub == 1, coef, 0.0)).T
    rinv_c = jnp.broadcast_to(scal[:, 0:1], (toks, hd))
    coef_c = jnp.broadcast_to(scal[:, 1:2], (toks, hd))

    def make_grad(h):
        g = (gdy[:, cols(h)] * rinv_c - attn[:, cols(h)] * coef_c).astype(BF16)
        go[:, cols(h)] = g
        own_x[h, :hd, :] = mm(ql_t[h], g)

    for j in range(half):
        make_grad(theirs[j])
        swap(own_x, sib_x, x_tx, x_rx, theirs[j], j).start()
    for j in range(half):
        make_grad(mine[j])

        @pl.when(second)
        def _():
            swap(own_x, sib_x, x_tx, x_rx, mine[j], half + j).start()

    for j in range(half):
        h = mine[j]
        swap(own_x, sib_x, x_tx, x_rx, h, j).wait_recv()
        l0, l1 = logs(h)
        a = own_x[h, :hd, :]
        b = sib_x[h, :hd, :]
        pass_x[j] = jnp.where(first, a, b) + jnp.exp(l0) * jnp.where(first, b, a)

        @pl.when(jnp.logical_not(has_next) & has_prev)
        def _():
            for i in range(CUTS):
                hop(pass_x, sgrad, f_tx, f_rx, j, i, -2).start()

    @pl.when(from_end == 1)
    def _():
        chain_back()

    for h in range(heads):
        g = go[:, cols(h)]
        w = (mm(g, v[:, cols(h)], 1, 1) * decay[h]).astype(BF16)
        out = mm(w, k[:, cols(h)]) + lead[h] * mm(g, s_in[h], 1, 1)
        gq[:, cols(h)] = out.astype(BF16)
        part_k[:, cols(h)] = mm(w, q[:, cols(h)], 0, 0)
        part_v[:, cols(h)] = mm(fwd_w[h], g, 0, 0)

    @pl.when(from_end > 1)
    def _():
        chain_back()

    @pl.when(first)
    def _():
        for j in range(half):
            swap(own_x, sib_x, x_tx, x_rx, theirs[j], half + j).wait_recv()

    for n, h in enumerate(mine + theirs):
        if n >= half:
            @pl.when(has_next)
            def _():
                for i in range(CUTS):
                    take(sgrad, d_tx, d_rx, n - half, i).wait_recv()

        @pl.when(second)
        def _():
            s_in[h] = sgrad[h].astype(BF16)

        @pl.when(first)
        def _():
            s_in[h] = (
                jnp.exp(sib_x[h, hd : hd + 1, :]) * sgrad[h] + sib_x[h, :hd, :]
            ).astype(BF16)

        f = s_in[h]
        gk[:, cols(h)] = (part_k[:, cols(h)] + tail[h] * mm(v[:, cols(h)], f, 1, 1)).astype(BF16)
        gv[:, cols(h)] = (part_v[:, cols(h)] + tail[h] * mm(k[:, cols(h)], f)).astype(BF16)

    for j in range(half):
        swap(own_s, sib_s, s_tx, s_rx, theirs[j], j).wait_send()
        swap(own_x, sib_x, x_tx, x_rx, theirs[j], j).wait_send()

        @pl.when(first)
        def _():
            swap(own_s, sib_s, s_tx, s_rx, mine[j], half + j).wait_send()

        @pl.when(second)
        def _():
            swap(own_x, sib_x, x_tx, x_rx, mine[j], half + j).wait_send()

    for d in range(1, nh):
        spread(d).wait_send()

    @pl.when(has_prev)
    def _():
        for j, i in pieces:
            give(state, c_tx, c_rx, j, i).wait_send()
            hop(pass_x, sgrad, f_tx, f_rx, j, i, -2).wait_send()

    @pl.when(has_next)
    def _():
        for j, i in pieces:
            give(sgrad, d_tx, d_rx, j, i).wait_send()
            hop(pass_s, state, e_tx, e_rx, j, i, 2).wait_send()


def hand_over(a, b, c, a_out, b_out, c_out, sem):
    moves = [
        pltpu.make_async_copy(src, dst, sem.at[i])
        for i, (src, dst) in enumerate(((a, a_out), (b, b_out), (c, c_out)))
    ]
    for one in moves:
        one.start()
    for one in moves:
        one.wait()


def on_device(queries, keys, values, log_decay, gain, grad_normed):
    toks, feats = queries.shape
    heads = log_decay.shape[1]
    hd = feats // heads
    half = heads // 2
    nz = lax.axis_size("ctx") // 2
    nh = lax.axis_size("head")
    vm = pl.BlockSpec(memory_space=pltpu.VMEM)
    hbm = pl.BlockSpec(memory_space=pltpu.HBM)
    dma = pltpu.SemaphoreType.DMA
    out = jax.ShapeDtypeStruct((toks, feats), BF16)
    others = max(nh - 1, 1)
    wide = pltpu.VMEM((toks, feats), BF16)
    wide32 = pltpu.VMEM((toks, feats), F32)
    per_head = pltpu.VMEM((heads, toks, hd), F32)
    tall = pltpu.VMEM((heads, hd + 8, hd), F32)
    full = pltpu.VMEM((heads, hd, hd), F32)
    part = pltpu.VMEM((half, hd, hd), F32)
    links = dma((half * CUTS,))
    scratch = [
        wide, wide, wide, pltpu.VMEM((heads, toks), F32), pltpu.VMEM((1, feats), F32), wide,
        tall, tall, full, part, tall, tall, full, part,
        pltpu.VMEM((8, toks), F32), pltpu.VMEM((others, 8, toks), F32),
        wide32, wide, pltpu.VMEM((heads, toks, toks), BF16),
        pltpu.VMEM((heads, toks, toks), F32), wide32, wide32, wide32,
        per_head, per_head, pltpu.VMEM((heads, hd, toks), BF16),
        pltpu.VMEM((heads, hd, hd), BF16), pltpu.VMEM((128, toks), F32),
        dma((6,)),
        dma((heads,)), dma((heads,)), links, links, links, links,
        dma((others,)), dma((others,)),
        dma((heads,)), dma((heads,)), links, links, links, links,
    ]
    grads = pl.pallas_call(
        functools.partial(kernel, nz, nh, heads * hd * nh),
        out_shape=(out, out, out),
        in_specs=[hbm] * 6,
        out_specs=(vm, vm, vm),
        scratch_shapes=scratch,
        compiler_params=pltpu.CompilerParams(
            collective_id=0, has_side_effects=True, vmem_limit_bytes=62464 * 1024
        ),
    )(queries, keys, values, log_decay.T, gain.reshape(1, feats), grad_normed)
    return pl.pallas_call(
        hand_over,
        out_shape=(out, out, out),
        in_specs=[vm] * 3,
        out_specs=(hbm, hbm, hbm),
        scratch_shapes=[dma((3,))],
    )(*grads)


def solution(mesh):
    in_specs = (
        P("ctx", "head"),
        P("ctx", "head"),
        P("ctx", "head"),
        P("ctx", "head"),
        P("head"),
        P("ctx", "head"),
    )
    out_specs = (P("ctx", "head"), P("ctx", "head"), P("ctx", "head"))
    return jax.shard_map(
        on_device, mesh=mesh, in_specs=in_specs, out_specs=out_specs, check_vma=False
    )
```

```python
import functools

import jax
import jax.numpy as jnp
from jax import lax
from jax.experimental import pallas as pl
from jax.experimental.pallas import tpu as pltpu
from jax.sharding import PartitionSpec as P

F32 = jnp.float32
BF16 = jnp.bfloat16
MESH = pl.DeviceIdType.MESH
CUTS = 4


def mm(a, b, ca=1, cb=0):
    return lax.dot_general(a, b, (((ca,), (cb,)), ((), ())), preferred_element_type=F32)


def kernel(
    nz, nh, feats_all,
    q_h, k_h, v_h, ld_h, gain_h, dy_h,
    gq_h, gk_h, gv_h,
    gq, gk, gv, out_sem,
    q, k, v, ld, gain, dy,
    own_s, sib_s, state, pass_s, own_x, sib_x, sgrad, pass_x, red_tx, red_rx,
    attn, go, fwd_w, decay, part_k, part_v, gdy, lead, tail, ql_t, s_in, cum_s,
    in_sem, s_tx, s_rx, e_tx, e_rx, c_tx, c_rx, r_tx, r_rx, x_tx, x_rx, f_tx, f_rx, d_tx, d_rx,
):
    toks = q.shape[0]
    heads = ld.shape[0]
    hd = q.shape[1] // heads
    half = heads // 2
    rows = hd // CUTS
    me = lax.axis_index("ctx")
    grp = lax.axis_index("head")
    z = me // 2
    c = me % 2
    sib = me + 1 - 2 * c
    first = c == 0
    second = c == 1
    has_prev = z > 0
    has_next = z < nz - 1
    from_end = nz - 1 - z

    loads = [
        pltpu.make_async_copy(a, b, in_sem.at[i])
        for i, (a, b) in enumerate(
            ((ld_h, ld), (k_h, k), (v_h, v), (q_h, q), (dy_h, dy), (gain_h, gain))
        )
    ]
    for one in loads:
        one.start()

    def cols(h):
        if isinstance(h, int):
            return slice(h * hd, (h + 1) * hd)
        return pl.ds(pl.multiple_of(h * hd, hd), hd)

    def copy(src, dst, tx, rx, where):
        return pltpu.make_async_remote_copy(
            src_ref=src, dst_ref=dst, send_sem=tx, recv_sem=rx,
            device_id=where, device_id_type=MESH,
        )

    barrier = pltpu.get_barrier_semaphore()
    pl.semaphore_signal(barrier, inc=1, device_id={"ctx": sib}, device_id_type=MESH)
    for step in (2, 2 * nz - 2):
        pl.semaphore_signal(
            barrier, inc=1, device_id={"ctx": lax.rem(me + step, 2 * nz)}, device_id_type=MESH
        )
    for d in range(1, nh):
        pl.semaphore_signal(
            barrier, inc=1, device_id={"head": lax.rem(grp + d, nh)}, device_id_type=MESH
        )

    theirs = [half * (1 - c) + j for j in range(half)]
    mine = [half * c + j for j in range(half)]

    row = lax.broadcasted_iota(jnp.int32, (toks, toks), 0)
    col = lax.broadcasted_iota(jnp.int32, (toks, toks), 1)
    lower = row >= col
    upper = jnp.where(row <= col, 1.0, 0.0).astype(BF16)
    cum_s[...] = jnp.zeros_like(cum_s)
    loads[0].wait()
    logd = ld[...]
    high = logd.astype(BF16)
    rest = logd - high.astype(F32)
    mid = rest.astype(BF16)
    low = (rest - mid.astype(F32)).astype(BF16)
    cum_t = mm(high, upper) + mm(mid, upper) + mm(low, upper)
    cum_s[:heads, :] = cum_t
    cum = cum_s[...].T
    last = cum[toks - 1 : toks, :]
    lead_all = jnp.exp(cum)
    tail_all = jnp.exp(last - cum)
    for h in range(heads):
        tail[h] = jnp.broadcast_to(tail_all[:, h : h + 1], (toks, hd))
        log_h = jnp.broadcast_to(last[:, h : h + 1], (8, hd))
        own_s[h, hd:, :] = log_h
        own_x[h, hd:, :] = log_h
    loads[1].wait()
    loads[2].wait()

    def make_state(h):
        kt = (k[:, cols(h)].astype(F32) * tail[h]).astype(BF16)
        own_s[h, :hd, :] = mm(kt, v[:, cols(h)], 0, 0)

    def swap(src, dst, tx, rx, h, slot):
        return copy(src.at[h], dst.at[h], tx.at[slot], rx.at[slot], {"ctx": sib})

    for j in range(half):
        make_state(theirs[j])
        if j == 0:
            pl.semaphore_wait(barrier, 2 + nh)
        swap(own_s, sib_s, s_tx, s_rx, theirs[j], j).start()
    for j in range(half):
        make_state(mine[j])

        @pl.when(first)
        def _():
            swap(own_s, sib_s, s_tx, s_rx, mine[j], half + j).start()

    @pl.when(jnp.logical_not(has_prev))
    def _():
        state[...] = jnp.zeros_like(state)

    @pl.when(jnp.logical_not(has_next))
    def _():
        sgrad[...] = jnp.zeros_like(sgrad)

    def logs(h):
        a = own_s[h, hd : hd + 1, :]
        b = sib_s[h, hd : hd + 1, :]
        return jnp.where(first, a, b), jnp.where(first, b, a)

    def hop(buf, dst, tx, rx, j, i, step):
        part = pl.ds(i * rows, rows)
        n = j * CUTS + i
        return copy(
            buf.at[j, part], dst.at[mine[j], part], tx.at[n], rx.at[n], {"ctx": me + step}
        )

    def give(buf, tx, rx, j, i):
        part = pl.ds(i * rows, rows)
        n = j * CUTS + i
        return copy(buf.at[mine[j], part], buf.at[mine[j], part], tx.at[n], rx.at[n], {"ctx": sib})

    def take(buf, tx, rx, j, i):
        part = pl.ds(i * rows, rows)
        n = j * CUTS + i
        return copy(
            buf.at[theirs[j], part], buf.at[theirs[j], part], tx.at[n], rx.at[n], {"ctx": sib}
        )

    pieces = [(j, i) for j in range(half) for i in range(CUTS)]

    def chain(buf, dst, tx, rx, g_tx, g_rx, step, onward):
        both = []
        for j in range(half):
            l0, l1 = logs(mine[j])
            both.append(jnp.exp(l0 + l1))
        for j, i in pieces:
            part = pl.ds(i * rows, rows)
            hop(buf, dst, tx, rx, j, i, step).wait_recv()

            @pl.when(onward)
            def _():
                buf[j, part, :] = both[j] * dst[mine[j], part, :] + buf[j, part, :]
                hop(buf, dst, tx, rx, j, i, step).start()

            give(dst, g_tx, g_rx, j, i).start()

    def chain_fwd():
        chain(pass_s, state, e_tx, e_rx, c_tx, c_rx, 2, has_next)

    def chain_back():
        chain(pass_x, sgrad, f_tx, f_rx, d_tx, d_rx, -2, has_prev)

    for j in range(half):
        h = mine[j]
        swap(own_s, sib_s, s_tx, s_rx, h, j).wait_recv()
        l0, l1 = logs(h)
        a = own_s[h, :hd, :]
        b = sib_s[h, :hd, :]
        pass_s[j] = jnp.exp(l1) * jnp.where(first, a, b) + jnp.where(first, b, a)

        @pl.when(jnp.logical_not(has_prev) & has_next)
        def _():
            for i in range(CUTS):
                hop(pass_s, state, e_tx, e_rx, j, i, 2).start()

    @pl.when(z == 1)
    def _():
        chain_fwd()

    for one in loads[3:]:
        one.wait()
    for h in range(heads):
        diff = cum[:, h : h + 1] - cum_t[h : h + 1, :]
        dec = jnp.where(lower, jnp.exp(jnp.minimum(diff, 0.0)), 0.0)
        decay[h] = dec
        w = (mm(q[:, cols(h)], k[:, cols(h)], 1, 1) * dec).astype(BF16)
        fwd_w[h] = w
        attn[:, cols(h)] = mm(w, v[:, cols(h)])
        ahead = jnp.broadcast_to(lead_all[:, h : h + 1], (toks, hd))
        lead[h] = ahead
        ql_t[h] = (q[:, cols(h)].astype(F32) * ahead).astype(BF16).T
        gdy[:, cols(h)] = gain[:, cols(h)] * dy[:, cols(h)].astype(F32)

    @pl.when(z > 1)
    def _():
        chain_fwd()

    @pl.when(second)
    def _():
        for j in range(half):
            swap(own_s, sib_s, s_tx, s_rx, theirs[j], half + j).wait_recv()

    sq = jnp.zeros((toks, hd), F32)
    cr = jnp.zeros((toks, hd), F32)
    for n, h in enumerate(mine + theirs):
        if n >= half:
            @pl.when(has_prev)
            def _():
                for i in range(CUTS):
                    take(state, c_tx, c_rx, n - half, i).wait_recv()

        @pl.when(first)
        def _():
            s_in[h] = state[h].astype(BF16)

        @pl.when(second)
        def _():
            s_in[h] = (
                jnp.exp(sib_s[h, hd : hd + 1, :]) * state[h] + sib_s[h, :hd, :]
            ).astype(BF16)

        a = attn[:, cols(h)] + lead[h] * mm(q[:, cols(h)], s_in[h])
        attn[:, cols(h)] = a
        sq = sq + a * a
        cr = cr + gdy[:, cols(h)] * a
    lane = lax.broadcasted_iota(jnp.int32, (toks, 128), 1)
    sq = jnp.sum(sq, axis=1, keepdims=True)
    cr = jnp.sum(cr, axis=1, keepdims=True)
    both = jnp.where(lane == 0, sq, jnp.where(lane == 1, cr, 0.0)).T
    red_tx[...] = both[:8, :]

    def spread(d):
        return copy(
            red_tx, red_rx.at[d - 1], r_tx.at[d - 1], r_rx.at[d - 1],
            {"head": lax.rem(grp + d, nh)},
        )

    for d in range(1, nh):
        spread(d).start()
    total = red_tx[...]
    for d in range(1, nh):
        spread(d).wait_recv()
        total = total + red_rx[d - 1]
    rinv = 1.0 / jnp.sqrt(total[0:1, :] / feats_all + 1e-06)
    coef = total[1:2, :] * (rinv * rinv * rinv) / feats_all
    sub = lax.broadcasted_iota(jnp.int32, (128, toks), 0)
    scal = jnp.where(sub == 0, rinv, jnp.where(sub == 1, coef, 0.0)).T
    rinv_c = jnp.broadcast_to(scal[:, 0:1], (toks, hd))
    coef_c = jnp.broadcast_to(scal[:, 1:2], (toks, hd))

    def make_grad(h):
        g = (gdy[:, cols(h)] * rinv_c - attn[:, cols(h)] * coef_c).astype(BF16)
        go[:, cols(h)] = g
        own_x[h, :hd, :] = mm(ql_t[h], g)

    for j in range(half):
        make_grad(theirs[j])
        swap(own_x, sib_x, x_tx, x_rx, theirs[j], j).start()
    for j in range(half):
        make_grad(mine[j])

        @pl.when(second)
        def _():
            swap(own_x, sib_x, x_tx, x_rx, mine[j], half + j).start()

    for j in range(half):
        h = mine[j]
        swap(own_x, sib_x, x_tx, x_rx, h, j).wait_recv()
        l0, l1 = logs(h)
        a = own_x[h, :hd, :]
        b = sib_x[h, :hd, :]
        pass_x[j] = jnp.where(first, a, b) + jnp.exp(l0) * jnp.where(first, b, a)

        @pl.when(jnp.logical_not(has_next) & has_prev)
        def _():
            for i in range(CUTS):
                hop(pass_x, sgrad, f_tx, f_rx, j, i, -2).start()

    @pl.when(from_end == 1)
    def _():
        chain_back()

    for h in range(heads):
        g = go[:, cols(h)]
        w = (mm(g, v[:, cols(h)], 1, 1) * decay[h]).astype(BF16)
        out = mm(w, k[:, cols(h)]) + lead[h] * mm(g, s_in[h], 1, 1)
        gq[:, cols(h)] = out.astype(BF16)
        part_k[:, cols(h)] = mm(w, q[:, cols(h)], 0, 0)
        part_v[:, cols(h)] = mm(fwd_w[h], g, 0, 0)
    stores = [pltpu.make_async_copy(gq, gq_h, out_sem.at[0])]
    stores[0].start()

    @pl.when(from_end > 1)
    def _():
        chain_back()

    @pl.when(first)
    def _():
        for j in range(half):
            swap(own_x, sib_x, x_tx, x_rx, theirs[j], half + j).wait_recv()

    for n, h in enumerate(mine + theirs):
        if n >= half:
            @pl.when(has_next)
            def _():
                for i in range(CUTS):
                    take(sgrad, d_tx, d_rx, n - half, i).wait_recv()

        @pl.when(second)
        def _():
            s_in[h] = sgrad[h].astype(BF16)

        @pl.when(first)
        def _():
            s_in[h] = (
                jnp.exp(sib_x[h, hd : hd + 1, :]) * sgrad[h] + sib_x[h, :hd, :]
            ).astype(BF16)

        f = s_in[h]
        gk[:, cols(h)] = (part_k[:, cols(h)] + tail[h] * mm(v[:, cols(h)], f, 1, 1)).astype(BF16)
        gv[:, cols(h)] = (part_v[:, cols(h)] + tail[h] * mm(k[:, cols(h)], f)).astype(BF16)
        for src, dst in ((gk, gk_h), (gv, gv_h)):
            one = pltpu.make_async_copy(
                src.at[:, cols(h)], dst.at[:, cols(h)], out_sem.at[len(stores)]
            )
            one.start()
            stores.append(one)

    for j in range(half):
        swap(own_s, sib_s, s_tx, s_rx, theirs[j], j).wait_send()
        swap(own_x, sib_x, x_tx, x_rx, theirs[j], j).wait_send()

        @pl.when(first)
        def _():
            swap(own_s, sib_s, s_tx, s_rx, mine[j], half + j).wait_send()

        @pl.when(second)
        def _():
            swap(own_x, sib_x, x_tx, x_rx, mine[j], half + j).wait_send()

    for one in stores:
        one.wait()
    for d in range(1, nh):
        spread(d).wait_send()

    @pl.when(has_prev)
    def _():
        for j, i in pieces:
            give(state, c_tx, c_rx, j, i).wait_send()
            hop(pass_x, sgrad, f_tx, f_rx, j, i, -2).wait_send()

    @pl.when(has_next)
    def _():
        for j, i in pieces:
            give(sgrad, d_tx, d_rx, j, i).wait_send()
            hop(pass_s, state, e_tx, e_rx, j, i, 2).wait_send()


def hand_over(a, b, c, a_out, b_out, c_out, held, in_sem, out_sem):
    ins = [
        pltpu.make_async_copy(src, held.at[i], in_sem.at[i]) for i, src in enumerate((a, b, c))
    ]
    outs = [
        pltpu.make_async_copy(held.at[i], dst, out_sem.at[i])
        for i, dst in enumerate((a_out, b_out, c_out))
    ]
    for one in ins:
        one.start()
    for got, put in zip(ins, outs):
        got.wait()
        put.start()
    for one in outs:
        one.wait()


def on_device(queries, keys, values, log_decay, gain, grad_normed):
    toks, feats = queries.shape
    heads = log_decay.shape[1]
    hd = feats // heads
    half = heads // 2
    nz = lax.axis_size("ctx") // 2
    nh = lax.axis_size("head")
    hbm = pl.BlockSpec(memory_space=pltpu.HBM)
    dma = pltpu.SemaphoreType.DMA
    out = jax.ShapeDtypeStruct((toks, feats), BF16)
    others = max(nh - 1, 1)
    wide = pltpu.VMEM((toks, feats), BF16)
    wide32 = pltpu.VMEM((toks, feats), F32)
    per_head = pltpu.VMEM((heads, toks, hd), F32)
    tall = pltpu.VMEM((heads, hd + 8, hd), F32)
    full = pltpu.VMEM((heads, hd, hd), F32)
    part = pltpu.VMEM((half, hd, hd), F32)
    links = dma((half * CUTS,))
    scratch = [
        wide, wide, wide, dma((1 + 2 * heads,)),
        wide, wide, wide, pltpu.VMEM((heads, toks), F32), pltpu.VMEM((1, feats), F32), wide,
        tall, tall, full, part, tall, tall, full, part,
        pltpu.VMEM((8, toks), F32), pltpu.VMEM((others, 8, toks), F32),
        wide32, wide, pltpu.VMEM((heads, toks, toks), BF16),
        pltpu.VMEM((heads, toks, toks), F32), wide32, wide32, wide32,
        per_head, per_head, pltpu.VMEM((heads, hd, toks), BF16),
        pltpu.VMEM((heads, hd, hd), BF16), pltpu.VMEM((128, toks), F32),
        dma((6,)),
        dma((heads,)), dma((heads,)), links, links, links, links,
        dma((others,)), dma((others,)),
        dma((heads,)), dma((heads,)), links, links, links, links,
    ]
    grads = pl.pallas_call(
        functools.partial(kernel, nz, nh, heads * hd * nh),
        out_shape=(out, out, out),
        in_specs=[hbm] * 6,
        out_specs=(hbm, hbm, hbm),
        scratch_shapes=scratch,
        compiler_params=pltpu.CompilerParams(
            collective_id=0, has_side_effects=True, vmem_limit_bytes=62464 * 1024
        ),
    )(queries, keys, values, log_decay.T, gain.reshape(1, feats), grad_normed)
    return pl.pallas_call(
        hand_over,
        out_shape=(out, out, out),
        in_specs=[hbm] * 3,
        out_specs=(hbm, hbm, hbm),
        scratch_shapes=[pltpu.VMEM((3, toks, feats), BF16), dma((3,)), dma((3,))],
        compiler_params=pltpu.CompilerParams(vmem_limit_bytes=62464 * 1024),
    )(*grads)


def solution(mesh):
    in_specs = (
        P("ctx", "head"),
        P("ctx", "head"),
        P("ctx", "head"),
        P("ctx", "head"),
        P("head"),
        P("ctx", "head"),
    )
    out_specs = (P("ctx", "head"), P("ctx", "head"), P("ctx", "head"))
    return jax.shard_map(
        on_device, mesh=mesh, in_specs=in_specs, out_specs=out_specs, check_vma=False
    )
```

```python
import functools

import jax
import jax.numpy as jnp
from jax import lax
from jax.experimental import pallas as pl
from jax.experimental.pallas import tpu as pltpu
from jax.sharding import PartitionSpec as P

F32 = jnp.float32
BF16 = jnp.bfloat16
MESH = pl.DeviceIdType.MESH
CUTS = 4


def mm(a, b, ca=1, cb=0):
    return lax.dot_general(a, b, (((ca,), (cb,)), ((), ())), preferred_element_type=F32)


def kernel(
    nz, nh, feats_all,
    q_h, k_h, v_h, ld_h, gain_h, dy_h,
    gq_h, gk_h, gv_h,
    gq, gk, gv, out_sem,
    q, k, v, ld, gain, dy,
    own_s, sib_s, state, pass_s, own_x, sib_x, sgrad, pass_x, red_tx, red_rx,
    attn, go, fwd_w, decay, part_k, part_v, gdy, lead, tail, ql_t, s_in, cum_s,
    in_sem, s_tx, s_rx, e_tx, e_rx, c_tx, c_rx, r_tx, r_rx, x_tx, x_rx, f_tx, f_rx, d_tx, d_rx,
):
    toks = q.shape[0]
    heads = ld.shape[0]
    hd = q.shape[1] // heads
    half = heads // 2
    rows = hd // CUTS
    me = lax.axis_index("ctx")
    grp = lax.axis_index("head")
    z = me // 2
    c = me % 2
    sib = me + 1 - 2 * c
    first = c == 0
    second = c == 1
    has_prev = z > 0
    has_next = z < nz - 1
    from_end = nz - 1 - z

    loads = [
        pltpu.make_async_copy(a, b, in_sem.at[i])
        for i, (a, b) in enumerate(
            ((ld_h, ld), (k_h, k), (v_h, v), (q_h, q), (dy_h, dy), (gain_h, gain))
        )
    ]
    for one in loads:
        one.start()

    def cols(h):
        if isinstance(h, int):
            return slice(h * hd, (h + 1) * hd)
        return pl.ds(pl.multiple_of(h * hd, hd), hd)

    def copy(src, dst, tx, rx, where):
        return pltpu.make_async_remote_copy(
            src_ref=src, dst_ref=dst, send_sem=tx, recv_sem=rx,
            device_id=where, device_id_type=MESH,
        )

    barrier = pltpu.get_barrier_semaphore()
    pl.semaphore_signal(barrier, inc=1, device_id={"ctx": sib}, device_id_type=MESH)
    for step in (2, 2 * nz - 2):
        pl.semaphore_signal(
            barrier, inc=1, device_id={"ctx": lax.rem(me + step, 2 * nz)}, device_id_type=MESH
        )
    for d in range(1, nh):
        pl.semaphore_signal(
            barrier, inc=1, device_id={"head": lax.rem(grp + d, nh)}, device_id_type=MESH
        )

    theirs = [half * (1 - c) + j for j in range(half)]
    mine = [half * c + j for j in range(half)]

    row = lax.broadcasted_iota(jnp.int32, (toks, toks), 0)
    col = lax.broadcasted_iota(jnp.int32, (toks, toks), 1)
    lower = row >= col
    upper = jnp.where(row <= col, 1.0, 0.0).astype(BF16)
    cum_s[...] = jnp.zeros_like(cum_s)
    loads[0].wait()
    logd = ld[...]
    high = logd.astype(BF16)
    rest = logd - high.astype(F32)
    mid = rest.astype(BF16)
    low = (rest - mid.astype(F32)).astype(BF16)
    cum_t = mm(high, upper) + mm(mid, upper) + mm(low, upper)
    cum_s[:heads, :] = cum_t
    cum = cum_s[...].T
    last = cum[toks - 1 : toks, :]
    lead_all = jnp.exp(cum)
    tail_all = jnp.exp(last - cum)
    for h in range(heads):
        tail[h] = jnp.broadcast_to(tail_all[:, h : h + 1], (toks, hd))
        log_h = jnp.broadcast_to(last[:, h : h + 1], (8, hd))
        own_s[h, hd:, :] = log_h
        own_x[h, hd:, :] = log_h
    loads[1].wait()
    loads[2].wait()

    def make_state(h):
        kt = (k[:, cols(h)].astype(F32) * tail[h]).astype(BF16)
        own_s[h, :hd, :] = mm(kt, v[:, cols(h)], 0, 0)

    def swap(src, dst, tx, rx, h, slot):
        return copy(src.at[h], dst.at[h], tx.at[slot], rx.at[slot], {"ctx": sib})

    for j in range(half):
        make_state(theirs[j])
        if j == 0:
            pl.semaphore_wait(barrier, 2 + nh)
        swap(own_s, sib_s, s_tx, s_rx, theirs[j], j).start()
    for j in range(half):
        make_state(mine[j])

        @pl.when(first)
        def _():
            swap(own_s, sib_s, s_tx, s_rx, mine[j], half + j).start()

    @pl.when(jnp.logical_not(has_prev))
    def _():
        state[...] = jnp.zeros_like(state)

    @pl.when(jnp.logical_not(has_next))
    def _():
        sgrad[...] = jnp.zeros_like(sgrad)

    def logs(h):
        a = own_s[h, hd : hd + 1, :]
        b = sib_s[h, hd : hd + 1, :]
        return jnp.where(first, a, b), jnp.where(first, b, a)

    def hop(buf, dst, tx, rx, j, i, step):
        part = pl.ds(i * rows, rows)
        n = j * CUTS + i
        return copy(
            buf.at[j, part], dst.at[mine[j], part], tx.at[n], rx.at[n], {"ctx": me + step}
        )

    def give(buf, tx, rx, j, i):
        part = pl.ds(i * rows, rows)
        n = j * CUTS + i
        return copy(buf.at[mine[j], part], buf.at[mine[j], part], tx.at[n], rx.at[n], {"ctx": sib})

    def take(buf, tx, rx, j, i):
        part = pl.ds(i * rows, rows)
        n = j * CUTS + i
        return copy(
            buf.at[theirs[j], part], buf.at[theirs[j], part], tx.at[n], rx.at[n], {"ctx": sib}
        )

    pieces = [(j, i) for j in range(half) for i in range(CUTS)]

    def chain(buf, dst, tx, rx, g_tx, g_rx, step, onward):
        both = []
        for j in range(half):
            l0, l1 = logs(mine[j])
            both.append(jnp.exp(l0 + l1))
        for j, i in pieces:
            part = pl.ds(i * rows, rows)
            hop(buf, dst, tx, rx, j, i, step).wait_recv()

            @pl.when(onward)
            def _():
                buf[j, part, :] = both[j] * dst[mine[j], part, :] + buf[j, part, :]
                hop(buf, dst, tx, rx, j, i, step).start()

            give(dst, g_tx, g_rx, j, i).start()

    def chain_fwd():
        chain(pass_s, state, e_tx, e_rx, c_tx, c_rx, 2, has_next)

    def chain_back():
        chain(pass_x, sgrad, f_tx, f_rx, d_tx, d_rx, -2, has_prev)

    for j in range(half):
        h = mine[j]
        swap(own_s, sib_s, s_tx, s_rx, h, j).wait_recv()
        l0, l1 = logs(h)
        a = own_s[h, :hd, :]
        b = sib_s[h, :hd, :]
        pass_s[j] = jnp.exp(l1) * jnp.where(first, a, b) + jnp.where(first, b, a)

        @pl.when(jnp.logical_not(has_prev) & has_next)
        def _():
            for i in range(CUTS):
                hop(pass_s, state, e_tx, e_rx, j, i, 2).start()

    @pl.when(z == 1)
    def _():
        chain_fwd()

    for one in loads[3:]:
        one.wait()
    for h in range(heads):
        diff = cum[:, h : h + 1] - cum_t[h : h + 1, :]
        dec = jnp.where(lower, jnp.exp(jnp.minimum(diff, 0.0)), 0.0)
        decay[h] = dec
        w = (mm(q[:, cols(h)], k[:, cols(h)], 1, 1) * dec).astype(BF16)
        fwd_w[h] = w
        attn[:, cols(h)] = mm(w, v[:, cols(h)])
        ahead = jnp.broadcast_to(lead_all[:, h : h + 1], (toks, hd))
        lead[h] = ahead
        ql_t[h] = (q[:, cols(h)].astype(F32) * ahead).astype(BF16).T
        gdy[:, cols(h)] = gain[:, cols(h)] * dy[:, cols(h)].astype(F32)

    @pl.when(z > 1)
    def _():
        chain_fwd()

    @pl.when(second)
    def _():
        for j in range(half):
            swap(own_s, sib_s, s_tx, s_rx, theirs[j], half + j).wait_recv()

    sq = jnp.zeros((toks, hd), F32)
    cr = jnp.zeros((toks, hd), F32)
    for n, h in enumerate(mine + theirs):
        if n >= half:
            @pl.when(has_prev)
            def _():
                for i in range(CUTS):
                    take(state, c_tx, c_rx, n - half, i).wait_recv()

        @pl.when(first)
        def _():
            s_in[h] = state[h].astype(BF16)

        @pl.when(second)
        def _():
            s_in[h] = (
                jnp.exp(sib_s[h, hd : hd + 1, :]) * state[h] + sib_s[h, :hd, :]
            ).astype(BF16)

        a = attn[:, cols(h)] + lead[h] * mm(q[:, cols(h)], s_in[h])
        attn[:, cols(h)] = a
        sq = sq + a * a
        cr = cr + gdy[:, cols(h)] * a
    lane = lax.broadcasted_iota(jnp.int32, (toks, 128), 1)
    sq = jnp.sum(sq, axis=1, keepdims=True)
    cr = jnp.sum(cr, axis=1, keepdims=True)
    both = jnp.where(lane == 0, sq, jnp.where(lane == 1, cr, 0.0)).T
    red_tx[...] = both[:8, :]

    def spread(d):
        return copy(
            red_tx, red_rx.at[d - 1], r_tx.at[d - 1], r_rx.at[d - 1],
            {"head": lax.rem(grp + d, nh)},
        )

    for d in range(1, nh):
        spread(d).start()
    total = red_tx[...]
    for d in range(1, nh):
        spread(d).wait_recv()
        total = total + red_rx[d - 1]
    rinv = 1.0 / jnp.sqrt(total[0:1, :] / feats_all + 1e-06)
    coef = total[1:2, :] * (rinv * rinv * rinv) / feats_all
    sub = lax.broadcasted_iota(jnp.int32, (128, toks), 0)
    scal = jnp.where(sub == 0, rinv, jnp.where(sub == 1, coef, 0.0)).T
    rinv_c = jnp.broadcast_to(scal[:, 0:1], (toks, hd))
    coef_c = jnp.broadcast_to(scal[:, 1:2], (toks, hd))

    def make_grad(h):
        g = (gdy[:, cols(h)] * rinv_c - attn[:, cols(h)] * coef_c).astype(BF16)
        go[:, cols(h)] = g
        own_x[h, :hd, :] = mm(ql_t[h], g)

    for j in range(half):
        make_grad(theirs[j])
        swap(own_x, sib_x, x_tx, x_rx, theirs[j], j).start()
    for j in range(half):
        make_grad(mine[j])

        @pl.when(second)
        def _():
            swap(own_x, sib_x, x_tx, x_rx, mine[j], half + j).start()

    for j in range(half):
        h = mine[j]
        swap(own_x, sib_x, x_tx, x_rx, h, j).wait_recv()
        l0, l1 = logs(h)
        a = own_x[h, :hd, :]
        b = sib_x[h, :hd, :]
        pass_x[j] = jnp.where(first, a, b) + jnp.exp(l0) * jnp.where(first, b, a)

        @pl.when(jnp.logical_not(has_next) & has_prev)
        def _():
            for i in range(CUTS):
                hop(pass_x, sgrad, f_tx, f_rx, j, i, -2).start()

    @pl.when(from_end == 1)
    def _():
        chain_back()

    for h in range(heads):
        g = go[:, cols(h)]
        w = (mm(g, v[:, cols(h)], 1, 1) * decay[h]).astype(BF16)
        out = mm(w, k[:, cols(h)]) + lead[h] * mm(g, s_in[h], 1, 1)
        gq[:, cols(h)] = out.astype(BF16)
        part_k[:, cols(h)] = mm(w, q[:, cols(h)], 0, 0)
        part_v[:, cols(h)] = mm(fwd_w[h], g, 0, 0)
    stores = [pltpu.make_async_copy(gq, gq_h, out_sem.at[0])]
    stores[0].start()

    @pl.when(from_end > 1)
    def _():
        chain_back()

    @pl.when(first)
    def _():
        for j in range(half):
            swap(own_x, sib_x, x_tx, x_rx, theirs[j], half + j).wait_recv()

    for n, h in enumerate(mine + theirs):
        if n >= half:
            @pl.when(has_next)
            def _():
                for i in range(CUTS):
                    take(sgrad, d_tx, d_rx, n - half, i).wait_recv()

        @pl.when(second)
        def _():
            s_in[h] = sgrad[h].astype(BF16)

        @pl.when(first)
        def _():
            s_in[h] = (
                jnp.exp(sib_x[h, hd : hd + 1, :]) * sgrad[h] + sib_x[h, :hd, :]
            ).astype(BF16)

        f = s_in[h]
        gk[:, cols(h)] = (part_k[:, cols(h)] + tail[h] * mm(v[:, cols(h)], f, 1, 1)).astype(BF16)
        gv[:, cols(h)] = (part_v[:, cols(h)] + tail[h] * mm(k[:, cols(h)], f)).astype(BF16)
        for src, dst in ((gk, gk_h), (gv, gv_h)):
            one = pltpu.make_async_copy(
                src.at[:, cols(h)], dst.at[:, cols(h)], out_sem.at[len(stores)]
            )
            one.start()
            stores.append(one)

    for j in range(half):
        swap(own_s, sib_s, s_tx, s_rx, theirs[j], j).wait_send()
        swap(own_x, sib_x, x_tx, x_rx, theirs[j], j).wait_send()

        @pl.when(first)
        def _():
            swap(own_s, sib_s, s_tx, s_rx, mine[j], half + j).wait_send()

        @pl.when(second)
        def _():
            swap(own_x, sib_x, x_tx, x_rx, mine[j], half + j).wait_send()

    for one in stores:
        one.wait()
    for d in range(1, nh):
        spread(d).wait_send()

    @pl.when(has_prev)
    def _():
        for j, i in pieces:
            give(state, c_tx, c_rx, j, i).wait_send()
            hop(pass_x, sgrad, f_tx, f_rx, j, i, -2).wait_send()

    @pl.when(has_next)
    def _():
        for j, i in pieces:
            give(sgrad, d_tx, d_rx, j, i).wait_send()
            hop(pass_s, state, e_tx, e_rx, j, i, 2).wait_send()


def hand_over(a, b, c, a_out, b_out, c_out, held, in_sem, out_sem):
    rows = a.shape[0] // 2
    ins, outs = [], []
    for n, (src, dst) in enumerate(((a, a_out), (b, b_out), (c, c_out))):
        for i in range(2):
            part = pl.ds(i * rows, rows)
            ins.append(
                pltpu.make_async_copy(src.at[part], held.at[n, part], in_sem.at[2 * n + i])
            )
            outs.append(
                pltpu.make_async_copy(held.at[n, part], dst.at[part], out_sem.at[2 * n + i])
            )
    for one in ins:
        one.start()
    for got, put in zip(ins, outs):
        got.wait()
        put.start()
    for one in outs:
        one.wait()


def on_device(queries, keys, values, log_decay, gain, grad_normed):
    toks, feats = queries.shape
    heads = log_decay.shape[1]
    hd = feats // heads
    half = heads // 2
    nz = lax.axis_size("ctx") // 2
    nh = lax.axis_size("head")
    hbm = pl.BlockSpec(memory_space=pltpu.HBM)
    dma = pltpu.SemaphoreType.DMA
    out = jax.ShapeDtypeStruct((toks, feats), BF16)
    others = max(nh - 1, 1)
    wide = pltpu.VMEM((toks, feats), BF16)
    wide32 = pltpu.VMEM((toks, feats), F32)
    per_head = pltpu.VMEM((heads, toks, hd), F32)
    tall = pltpu.VMEM((heads, hd + 8, hd), F32)
    full = pltpu.VMEM((heads, hd, hd), F32)
    part = pltpu.VMEM((half, hd, hd), F32)
    links = dma((half * CUTS,))
    scratch = [
        wide, wide, wide, dma((1 + 2 * heads,)),
        wide, wide, wide, pltpu.VMEM((heads, toks), F32), pltpu.VMEM((1, feats), F32), wide,
        tall, tall, full, part, tall, tall, full, part,
        pltpu.VMEM((8, toks), F32), pltpu.VMEM((others, 8, toks), F32),
        wide32, wide, pltpu.VMEM((heads, toks, toks), BF16),
        pltpu.VMEM((heads, toks, toks), F32), wide32, wide32, wide32,
        per_head, per_head, pltpu.VMEM((heads, hd, toks), BF16),
        pltpu.VMEM((heads, hd, hd), BF16), pltpu.VMEM((128, toks), F32),
        dma((6,)),
        dma((heads,)), dma((heads,)), links, links, links, links,
        dma((others,)), dma((others,)),
        dma((heads,)), dma((heads,)), links, links, links, links,
    ]
    grads = pl.pallas_call(
        functools.partial(kernel, nz, nh, heads * hd * nh),
        out_shape=(out, out, out),
        in_specs=[hbm] * 6,
        out_specs=(hbm, hbm, hbm),
        scratch_shapes=scratch,
        compiler_params=pltpu.CompilerParams(
            collective_id=0, has_side_effects=True, vmem_limit_bytes=62464 * 1024
        ),
    )(queries, keys, values, log_decay.T, gain.reshape(1, feats), grad_normed)
    return pl.pallas_call(
        hand_over,
        out_shape=(out, out, out),
        in_specs=[hbm] * 3,
        out_specs=(hbm, hbm, hbm),
        scratch_shapes=[pltpu.VMEM((3, toks, feats), BF16), dma((6,)), dma((6,))],
        compiler_params=pltpu.CompilerParams(vmem_limit_bytes=62464 * 1024),
    )(*grads)


def solution(mesh):
    in_specs = (
        P("ctx", "head"),
        P("ctx", "head"),
        P("ctx", "head"),
        P("ctx", "head"),
        P("head"),
        P("ctx", "head"),
    )
    out_specs = (P("ctx", "head"), P("ctx", "head"), P("ctx", "head"))
    return jax.shard_map(
        on_device, mesh=mesh, in_specs=in_specs, out_specs=out_specs, check_vma=False
    )
```
